32 devices in a mesh: chan: 8 (over y, x, core), win: 4 (over z).
Axes of the slice: x: 2, y: 2, z: 4, core: 2. Of those that a mesh axis runs over, the one named last changes fastest.
Arguments:
- records: bfloat16 [4, 128, 7680], P('win', 'chan'), may hold values from -6 to 6
- source_rows: int32 [1, 256], replicated, may hold values from 0 to 15
Outputs:
- correlation: float32 [256, 128, 2048], P(None, ('chan', 'win'))
The draws below stay inside these ranges and needn't reach their ends.
Inputs may be any that keep to these rules, and one draw needn't show every extreme that they name: Entry j of row b of source_rows names a channel of channel shard j // 32, counted within that shard; entries may repeat.
All inputs are finite; a program needn't handle non-finite values.
Results may differ from the reference program's by a relative error of at most 0.0063.
Values may be sent and summed in bfloat16 or wider, within the bound.
A program may use at most 64 MiB of HBM per device.

```python
import math
import jax
import jax.numpy as jnp
from jax import lax

S = 7680
NBINS = 512
HALF = 32
FIRST_BIN = 64
MAXLAG = 1024
BLOCK = 256
R_DEV = 16
STEPS = 1
CHANNELS = 128
WINDOWS = 4
SOURCES = 256
N_CHAN = 8


def with_ends(values, own_key, least, top_value):
    place = [jax.random.randint(jax.random.fold_in(own_key, axis), (), 0, length) for axis, length in enumerate(values.shape)]
    widest = values.shape.index(max(values.shape))
    neighbour = place[:widest] + [(place[widest] + 1) % values.shape[widest]] + place[widest + 1:]
    return values.at[tuple(place)].set(least).at[tuple(neighbour)].set(top_value)


def level_of(own_key, dims, split, low, top_value):
    gain = 1.0
    for position, shards_of in split:
        steps = jax.random.uniform(jax.random.fold_in(jax.random.fold_in(own_key, 6), position), (shards_of,), jnp.float32, low / len(split), top_value / len(split))
        gain = gain * jnp.repeat(jnp.exp(steps), dims[position] // shards_of).reshape((-1,) + (1,) * (len(dims) - 1 - position))
    return gain


def noise(stream_key, shape, spread, reach, shards=(), held_as=jnp.bfloat16):
    values = spread * jax.random.normal(stream_key, shape, jnp.float32)
    if shards:
        values = values * level_of(stream_key, shape, shards, -0.22, 0.18)
    return jnp.clip(values, -reach, reach).astype(held_as)


def setup_inputs(seed: int = 0) -> dict:
    arg_keys = jax.random.split(jax.random.key(seed), 3)
    records = noise(arg_keys[0], (WINDOWS, CHANNELS, S), 1.0, 6.0, ((0, 4), (1, 8)))
    source_rows = with_ends(jax.random.randint(arg_keys[1], (STEPS, BLOCK), 0, R_DEV), jax.random.fold_in(arg_keys[1], 1), 0, R_DEV - 1).astype(jnp.int32)
    return dict(records=records, source_rows=source_rows)


full_turn = 2.0 * math.pi

def band_table():
    bin_ids = FIRST_BIN - HALF + jnp.arange(NBINS + 2 * HALF, dtype=jnp.int32)
    sample_ids = jnp.arange(S, dtype=jnp.int32)
    angles = (sample_ids[:, None] * bin_ids[None, :] % S).astype(jnp.float32) * (full_turn / S)
    return jnp.concatenate([jnp.cos(angles), -jnp.sin(angles)], axis=1).astype(jnp.bfloat16)

def lag_weights():
    bin_ids = FIRST_BIN + jnp.arange(NBINS, dtype=jnp.int32)
    lag_ids = jnp.arange(2 * MAXLAG, dtype=jnp.int32) - MAXLAG
    angles = (bin_ids[:, None] * lag_ids[None, :] % S).astype(jnp.float32) * (full_turn / S)
    return jnp.concatenate([jnp.cos(angles), -jnp.sin(angles)], axis=0).astype(jnp.bfloat16)

def normalize(spectrum):
    extent = NBINS + 2 * HALF
    real_part = spectrum[:, :extent]
    imag_part = spectrum[:, extent:]
    magnitude = jnp.sqrt(real_part * real_part + imag_part * imag_part)
    smooth = magnitude[:, 0:NBINS]
    for offset in range(1, 2 * HALF + 1):
        smooth = smooth + magnitude[:, offset:offset + NBINS]
    smooth = smooth / (2 * HALF + 1) + 1e-06
    centre_re = real_part[:, HALF:HALF + NBINS] / smooth
    centre_im = imag_part[:, HALF:HALF + NBINS] / smooth
    return jnp.stack([centre_re, centre_im], axis=1).astype(jnp.bfloat16)

def cross_terms(source_part, receiver_part):
    first = source_part.astype(jnp.float32)
    second = receiver_part.astype(jnp.float32)
    real_sum = jnp.einsum('wbi,wri->bri', first[:, :, 0], second[:, :, 0]) + jnp.einsum('wbi,wri->bri', first[:, :, 1], second[:, :, 1])
    imag_sum = jnp.einsum('wbi,wri->bri', first[:, :, 1], second[:, :, 0]) - jnp.einsum('wbi,wri->bri', first[:, :, 0], second[:, :, 1])
    return jnp.stack([real_sum, imag_sum], axis=2)

def reference(records, source_rows):
    flat = records.reshape(WINDOWS * CHANNELS, S)
    whitened = normalize(jnp.dot(flat, band_table(), preferred_element_type=jnp.float32))
    whitened = whitened.reshape(WINDOWS, CHANNELS, 2, NBINS)
    per_shard = BLOCK // N_CHAN
    base_rows = jnp.arange(BLOCK, dtype=jnp.int32) // per_shard * R_DEV
    source_index = (base_rows[None, :] + source_rows).astype(jnp.int32)
    picked = jnp.take(whitened, source_index.reshape(-1), axis=1)
    grouped = picked.reshape(WINDOWS, SOURCES // 8, 8, 2, NBINS).transpose(1, 0, 2, 3, 4)
    weights = lag_weights()
    lag_scale = math.sqrt(2.0 / (WINDOWS * NBINS))

    def per_group(member):
        spectra = cross_terms(member, whitened)
        rounded = spectra.astype(jnp.bfloat16).reshape(8 * CHANNELS, 2 * NBINS)
        result = jnp.dot(rounded, weights, preferred_element_type=jnp.float32) * lag_scale
        return result.reshape(8, CHANNELS, 2 * MAXLAG)
    outcome = lax.map(per_group, grouped)
    return outcome.reshape(SOURCES, CHANNELS, 2 * MAXLAG)
```

```python
import functools
import math

import jax
import jax.numpy as jnp
import ml_dtypes
import numpy as np
from jax import lax
from jax.experimental import pallas as pl
from jax.experimental.pallas import tpu as pltpu
from jax.sharding import PartitionSpec as P

S = 7680
NBINS = 512
HALF = 32
FIRST_BIN = 64
MAXLAG = 1024

INNER = 512
OUTER = S // INNER
LOW = FIRST_BIN - HALF
WIDE = 640
CB = 64
LANES = 128
GROUPS = 2 * MAXLAG // LANES
MESH = pl.DeviceIdType.MESH
bf16 = jnp.bfloat16
f32 = jnp.float32


def angles(left, right):
    turn = np.float32(2.0 * math.pi / S)
    return (left[:, None] * right[None, :] % S).astype(np.float32) * turn


def inner_table():
    a = angles(np.arange(INNER), LOW + np.arange(WIDE))
    return np.concatenate([np.cos(a), -np.sin(a)], axis=1).astype(ml_dtypes.bfloat16)


def outer_table():
    a = angles(INNER * np.arange(OUTER), LOW + np.arange(WIDE))
    return np.stack([np.cos(a), np.sin(a)]).astype(np.float32)


def lag_table():
    a = angles(FIRST_BIN + np.arange(NBINS), np.arange(2 * MAXLAG) - MAXLAG)
    return np.concatenate([np.cos(a), -np.sin(a)], axis=0).astype(ml_dtypes.bfloat16)


def spectra_of(x_ref, table_ref, outer_ref):
    rows = x_ref.shape[0]
    parts = [x_ref[:, i * INNER : (i + 1) * INNER] for i in range(OUTER)]
    z = jnp.dot(
        jnp.concatenate(parts, axis=0), table_ref[...], preferred_element_type=f32
    )
    re = im = None
    for i in range(OUTER):
        zr = z[i * rows : (i + 1) * rows, :WIDE]
        zi = z[i * rows : (i + 1) * rows, WIDE:]
        c = outer_ref[0, i : i + 1, :]
        s = outer_ref[1, i : i + 1, :]
        tr = zr * c + zi * s
        ti = zi * c - zr * s
        re = tr if re is None else re + tr
        im = ti if im is None else im + ti
    return re, im


def whiten(re, im):
    total = jnp.sqrt(re * re + im * im)
    first = total
    span = 1
    while span < 2 * HALF:
        total = total + pltpu.roll(total, WIDE - span, 1)
        span *= 2
    total = total + pltpu.roll(first, WIDE - span, 1)
    amplitude = total[:, :NBINS] / (2 * HALF + 1) + 1e-06
    re = pltpu.roll(re, WIDE - HALF, 1)[:, :NBINS] / amplitude
    im = pltpu.roll(im, WIDE - HALF, 1)[:, :NBINS] / amplitude
    return re.astype(bf16), im.astype(bf16)


def gather_kernel(
    n_win, n_chan, x_ref, table_ref, outer_ref, all_ref, s1, r1, s2, r2, s3, r3
):
    rows = x_ref.shape[0]
    chips = n_chan // 2
    win, chan = lax.axis_index("win"), lax.axis_index("chan")
    chip, core = chan // 2, chan % 2
    sibling = chip * 2 + (1 - core)

    def turn(d):
        return lax.rem(win + d, n_win)

    def peer(p):
        return lax.rem(chip + p, chips) * 2 + core

    barrier = pltpu.get_barrier_semaphore()
    friends = [(chan, turn(d)) for d in range(1, n_win)]
    friends += [(peer(p), win) for p in range(1, chips)] + [(sibling, win)]
    for c, w in friends:
        pl.semaphore_signal(
            barrier, inc=1, device_id={"chan": c, "win": w}, device_id_type=MESH
        )

    re, im = whiten(*spectra_of(x_ref, table_ref, outer_ref))
    mine = pl.ds(pl.multiple_of(chan * rows, rows), rows)
    all_ref[win, mine, :NBINS] = re
    all_ref[win, mine, NBINS:] = im
    pl.semaphore_wait(barrier, len(friends))

    def copy(w, c, to_c, to_w, send, recv):
        block = all_ref.at[w, pl.ds(pl.multiple_of(c * rows, rows), rows)]
        return pltpu.make_async_remote_copy(
            src_ref=block,
            dst_ref=block,
            send_sem=send,
            recv_sem=recv,
            device_id={"chan": to_c, "win": to_w},
            device_id_type=MESH,
        )

    along_win = [
        copy(win, chan, chan, turn(d), s1.at[d], r1.at[d]) for d in range(1, n_win)
    ]
    for c in along_win:
        c.start()
    across, to_sibling = {}, {}
    for d in range(n_win):
        w = turn(n_win - d)
        if d:
            copy(w, chan, chan, turn(d), s1.at[d], r1.at[d]).wait_recv()
        for p in range(1, chips):
            across[d, p] = copy(w, chan, peer(p), win, s2.at[d, p], r2.at[d, p])
            across[d, p].start()
        to_sibling[d, 0] = copy(w, chan, sibling, win, s3.at[d, 0], r3.at[d, 0])
        to_sibling[d, 0].start()
    for d in range(n_win):
        w = turn(n_win - d)
        for p in range(1, chips):
            c = peer(chips - p)
            copy(w, c, peer(p), win, s2.at[d, p], r2.at[d, p]).wait_recv()
            to_sibling[d, p] = copy(w, c, sibling, win, s3.at[d, p], r3.at[d, p])
            to_sibling[d, p].start()
    for d in range(n_win):
        w = turn(n_win - d)
        for p in range(chips):
            c = lax.rem(chip + chips - p, chips) * 2 + (1 - core)
            copy(w, c, sibling, win, s3.at[d, p], r3.at[d, p]).wait_recv()
    for c in along_win + list(across.values()) + list(to_sibling.values()):
        c.wait_send()


def gathered(records, n_win, n_chan):
    rows = records.shape[0]
    chips = n_chan // 2
    vmem = pl.BlockSpec(memory_space=pltpu.VMEM)
    dma = pltpu.SemaphoreType.DMA
    return pl.pallas_call(
        functools.partial(gather_kernel, n_win, n_chan),
        out_shape=jax.ShapeDtypeStruct((n_win, n_chan * rows, 2 * NBINS), bf16),
        in_specs=[vmem] * 3,
        out_specs=vmem,
        scratch_shapes=[dma((n_win,))] * 2 + [dma((n_win, chips))] * 4,
        compiler_params=pltpu.CompilerParams(
            collective_id=0, has_side_effects=True, vmem_limit_bytes=40 * 2**20
        ),
        name="gather_spectra",
    )(records, jnp.asarray(inner_table()), jnp.asarray(outer_table()))


def stack_kernel(
    rows, per_shard, scale, all_ref, lag_ref, src_ref, out_ref, own, wide, lhs, corr, sem
):
    n_win, channels, _ = all_ref.shape
    n_rec = rows // n_win
    blocks = channels // CB
    sources = CB // rows * per_shard
    size = CB * GROUPS * n_rec
    lines = GROUPS * n_rec
    chan, win = lax.axis_index("chan"), lax.axis_index("win")
    for w in range(n_win):
        own[w] = all_ref[w, pl.ds(pl.multiple_of(chan * rows, rows), rows), :].astype(f32)
    for w in range(n_win):
        for r in range(n_rec):
            line = own[w, pl.ds(win * n_rec + r, 1), :]
            wide[w, r] = jnp.broadcast_to(line, (16, 2 * NBINS))

    def finish(slot):
        part = out_ref.at[pl.ds(0, sources * lines)]
        pltpu.make_async_copy(part, part, sem.at[slot]).wait()

    @pl.loop(0, blocks)
    def _(b):
        slot = lax.rem(b, 2)

        @pl.when(b >= 2)
        def _():
            finish(slot)

        for k in range(NBINS // LANES):
            at_re = pl.ds(k * LANES, LANES)
            at_im = pl.ds(NBINS + k * LANES, LANES)

            @pl.loop(0, CB // 16)
            def _(i):
                here = pl.ds(pl.multiple_of(b * CB + i * 16, 16), 16)
                s_re = [all_ref[w, here, at_re].astype(f32) for w in range(n_win)]
                s_im = [all_ref[w, here, at_im].astype(f32) for w in range(n_win)]
                for r in range(n_rec):
                    re = im = None
                    for w in range(n_win):
                        r_re, r_im = wide[w, r, :, at_re], wide[w, r, :, at_im]
                        a = s_re[w] * r_re + s_im[w] * r_im
                        c = s_im[w] * r_re - s_re[w] * r_im
                        re = a if re is None else re + a
                        im = c if im is None else im + c
                    to = pl.ds(pl.multiple_of(r * CB + i * 16, 16), 16)
                    lhs[to, at_re] = re.astype(bf16)
                    lhs[to, at_im] = im.astype(bf16)

        for n in range(GROUPS // 2):
            res = jnp.dot(
                lhs[...], lag_ref[:, n * 256 : (n + 1) * 256], preferred_element_type=f32
            )
            res = res * scale
            for h in range(2):
                for r in range(n_rec):
                    for c in range(0, CB, 8):
                        first = slot * size + (c * lines + (2 * n + h) * n_rec + r)
                        corr[pl.ds(first, 8, stride=lines), :] = res[
                            r * CB + c : r * CB + c + 8, h * LANES : (h + 1) * LANES
                        ]

        @pl.loop(0, sources)
        def _(i):
            j = b * sources + i
            c = i // per_shard * rows + src_ref[0, j]
            pltpu.make_async_copy(
                corr.at[pl.ds(pl.multiple_of(slot * size + c * lines, lines), lines)],
                out_ref.at[pl.ds(pl.multiple_of(j * lines, lines), lines)],
                sem.at[slot],
            ).start()

    for b in range(max(0, blocks - 2), blocks):
        finish(b % 2)


def stacked(everything, source_rows, rows, n_chan):
    n_win, channels, _ = everything.shape
    n_rec = rows // n_win
    count = source_rows.shape[1]
    scale = math.sqrt(2.0 / (n_win * NBINS))
    vmem = pl.BlockSpec(memory_space=pltpu.VMEM)
    out = pl.pallas_call(
        functools.partial(stack_kernel, rows, count // n_chan, scale),
        out_shape=jax.ShapeDtypeStruct((count * GROUPS * n_rec, LANES), f32),
        in_specs=[vmem, vmem, pl.BlockSpec(memory_space=pltpu.SMEM)],
        out_specs=pl.BlockSpec(memory_space=pl.ANY),
        scratch_shapes=[
            pltpu.VMEM((n_win, rows, 2 * NBINS), f32),
            pltpu.VMEM((n_win, n_rec, 16, 2 * NBINS), f32),
            pltpu.VMEM((n_rec * CB, 2 * NBINS), bf16),
            pltpu.VMEM((2 * CB * GROUPS * n_rec, LANES), f32),
            pltpu.SemaphoreType.DMA((2,)),
        ],
        compiler_params=pltpu.CompilerParams(vmem_limit_bytes=40 * 2**20),
        name="stack_correlations",
    )(everything, jnp.asarray(lag_table()), source_rows)
    out = out.reshape(count, GROUPS, n_rec, LANES).transpose(0, 2, 1, 3)
    return out.reshape(count, n_rec, 2 * MAXLAG)


def per_device(records, source_rows):
    n_win, n_chan = lax.axis_size("win"), lax.axis_size("chan")
    _, rows, samples = records.shape
    everything = gathered(records.reshape(rows, samples), n_win, n_chan)
    return stacked(everything, source_rows, rows, n_chan)


def solution(mesh):
    in_specs = (P("win", "chan", None), P())
    out_specs = P(None, ("chan", "win"), None)
    return jax.shard_map(
        per_device, mesh=mesh, in_specs=in_specs, out_specs=out_specs, check_vma=False
    )
```

```python
import functools
import math

import jax
import jax.numpy as jnp
import ml_dtypes
import numpy as np
from jax import lax
from jax.experimental import pallas as pl
from jax.experimental.pallas import tpu as pltpu
from jax.sharding import PartitionSpec as P

S = 7680
NBINS = 512
HALF = 32
FIRST_BIN = 64
MAXLAG = 1024

INNER = 512
OUTER = S // INNER
LOW = FIRST_BIN - HALF
WIDE = 640
LANES = 128
GROUPS = 2 * MAXLAG // LANES
MESH = pl.DeviceIdType.MESH
bf16 = jnp.bfloat16
f32 = jnp.float32


def angles(left, right):
    turn = np.float32(2.0 * math.pi / S)
    return (left[:, None] * right[None, :] % S).astype(np.float32) * turn


def inner_table():
    a = angles(np.arange(INNER), LOW + np.arange(WIDE))
    return np.concatenate([np.cos(a), -np.sin(a)], axis=1).astype(ml_dtypes.bfloat16)


def outer_table():
    a = angles(INNER * np.arange(OUTER), LOW + np.arange(WIDE))
    return np.stack([np.cos(a), np.sin(a)]).astype(np.float32)


def lag_table():
    a = angles(FIRST_BIN + np.arange(NBINS), np.arange(2 * MAXLAG) - MAXLAG)
    return np.concatenate([np.cos(a), -np.sin(a)], axis=0).astype(ml_dtypes.bfloat16)


def spectra_of(x_ref, table_ref, outer_ref):
    rows = x_ref.shape[0]
    parts = [x_ref[:, i * INNER : (i + 1) * INNER] for i in range(OUTER)]
    z = jnp.dot(
        jnp.concatenate(parts, axis=0), table_ref[...], preferred_element_type=f32
    )
    re = im = None
    for i in range(OUTER):
        zr = z[i * rows : (i + 1) * rows, :WIDE]
        zi = z[i * rows : (i + 1) * rows, WIDE:]
        c = outer_ref[0, i : i + 1, :]
        s = outer_ref[1, i : i + 1, :]
        tr = zr * c + zi * s
        ti = zi * c - zr * s
        re = tr if re is None else re + tr
        im = ti if im is None else im + ti
    return re, im


def whiten(re, im):
    total = jnp.sqrt(re * re + im * im)
    first = total
    span = 1
    while span < 2 * HALF:
        total = total + pltpu.roll(total, WIDE - span, 1)
        span *= 2
    total = total + pltpu.roll(first, WIDE - span, 1)
    amplitude = total[:, :NBINS] / (2 * HALF + 1) + 1e-06
    re = pltpu.roll(re, WIDE - HALF, 1)[:, :NBINS] / amplitude
    im = pltpu.roll(im, WIDE - HALF, 1)[:, :NBINS] / amplitude
    return re.astype(bf16), im.astype(bf16)


def correlate_kernel(
    n_win,
    n_chan,
    rows,
    scale,
    x_hbm,
    table_hbm,
    outer_hbm,
    lag_hbm,
    corr,
    x_ref,
    table_ref,
    outer_ref,
    lag_ref,
    all_ref,
    own,
    wide,
    lhs,
    load,
    s1,
    r1,
    s2,
    r2,
    s3,
    r3,
):
    chips = n_chan // 2
    n_rec = rows // n_win
    lines = GROUPS * n_rec
    per_chip = 2 * rows
    win, chan = lax.axis_index("win"), lax.axis_index("chan")
    chip, core = chan // 2, chan % 2
    sibling = chip * 2 + (1 - core)

    loads = [
        pltpu.make_async_copy(src, dst, load.at[i])
        for i, (src, dst) in enumerate(
            (
                (x_hbm, x_ref),
                (table_hbm, table_ref),
                (outer_hbm, outer_ref),
                (lag_hbm, lag_ref),
            )
        )
    ]
    for c in loads:
        c.start()

    def turn(d):
        return lax.rem(win + d, n_win)

    def peer(p):
        return lax.rem(chip + p, chips) * 2 + core

    barrier = pltpu.get_barrier_semaphore()
    friends = [(chan, turn(d)) for d in range(1, n_win)]
    friends += [(peer(p), win) for p in range(1, chips)] + [(sibling, win)]
    for c, w in friends:
        pl.semaphore_signal(
            barrier, inc=1, device_id={"chan": c, "win": w}, device_id_type=MESH
        )

    for c in loads[:3]:
        c.wait()
    re, im = whiten(*spectra_of(x_ref, table_ref, outer_ref))
    mine = pl.ds(pl.multiple_of(chan * rows, rows), rows)
    all_ref[win, mine, :NBINS] = re
    all_ref[win, mine, NBINS:] = im
    pl.semaphore_wait(barrier, len(friends))

    def copy(w, c, to_c, to_w, send, recv):
        block = all_ref.at[w, pl.ds(pl.multiple_of(c * rows, rows), rows)]
        return pltpu.make_async_remote_copy(
            src_ref=block,
            dst_ref=block,
            send_sem=send,
            recv_sem=recv,
            device_id={"chan": to_c, "win": to_w},
            device_id_type=MESH,
        )

    def along(d):
        return copy(win, chan, chan, turn(d), s1.at[d], r1.at[d])

    def across(d, p):
        return copy(turn(n_win - d), chan, peer(p), win, s2.at[d, p], r2.at[d, p])

    def onward(d, p):
        w, c = turn(n_win - d), peer(chips - p)
        return copy(w, c, sibling, win, s3.at[d, p], r3.at[d, p])

    for d in range(1, n_win):
        along(d).start()
    for d in range(n_win):
        if d:
            copy(turn(n_win - d), chan, chan, turn(d), s1.at[d], r1.at[d]).wait_recv()
        for p in range(1, chips):
            across(d, p).start()
        onward(d, 0).start()

    for w in range(n_win):
        own[w] = all_ref[w, mine, :].astype(f32)
    for w in range(n_win):
        for r in range(n_rec):
            line = own[w, pl.ds(win * n_rec + r, 1), :]
            wide[w, r] = jnp.broadcast_to(line, (16, 2 * NBINS))
    loads[3].wait()

    @pl.loop(1, chips + 1)
    def _(q):
        @pl.when(q < chips)
        def _():
            for d in range(n_win):
                w, c = turn(n_win - d), peer(chips - q)
                copy(w, c, peer(q), win, s2.at[d, q], r2.at[d, q]).wait_recv()
                onward(d, q).start()

        p = q - 1
        there = lax.rem(chip + chips - p, chips)
        for d in range(n_win):
            w, c = turn(n_win - d), there * 2 + (1 - core)
            copy(w, c, sibling, win, s3.at[d, p], r3.at[d, p]).wait_recv()

        for k in range(NBINS // LANES):
            at_re = pl.ds(k * LANES, LANES)
            at_im = pl.ds(NBINS + k * LANES, LANES)

            @pl.loop(0, per_chip // 16)
            def _(i):
                here = pl.ds(pl.multiple_of(there * per_chip + i * 16, 16), 16)
                s_re = [all_ref[w, here, at_re].astype(f32) for w in range(n_win)]
                s_im = [all_ref[w, here, at_im].astype(f32) for w in range(n_win)]
                for r in range(n_rec):
                    re = im = None
                    for w in range(n_win):
                        r_re, r_im = wide[w, r, :, at_re], wide[w, r, :, at_im]
                        a = s_re[w] * r_re + s_im[w] * r_im
                        c = s_im[w] * r_re - s_re[w] * r_im
                        re = a if re is None else re + a
                        im = c if im is None else im + c
                    to = pl.ds(pl.multiple_of(r * per_chip + i * 16, 16), 16)
                    lhs[to, at_re] = re.astype(bf16)
                    lhs[to, at_im] = im.astype(bf16)

        for n in range(GROUPS // 2):
            res = jnp.dot(
                lhs[...], lag_ref[:, n * 256 : (n + 1) * 256], preferred_element_type=f32
            )
            res = res * scale
            for h in range(2):
                for r in range(n_rec):
                    for c in range(0, per_chip, 8):
                        first = (there * per_chip + c) * lines + (2 * n + h) * n_rec + r
                        corr[pl.ds(first, 8, stride=lines), :] = res[
                            r * per_chip + c : r * per_chip + c + 8,
                            h * LANES : (h + 1) * LANES,
                        ]

    for d in range(1, n_win):
        along(d).wait_send()

    @pl.loop(1, chips)
    def _(p):
        for d in range(n_win):
            across(d, p).wait_send()

    @pl.loop(0, chips)
    def _(p):
        for d in range(n_win):
            onward(d, p).wait_send()


def correlated(records, n_win, n_chan):
    rows, samples = records.shape
    chips = n_chan // 2
    n_rec = rows // n_win
    channels = n_chan * rows
    scale = math.sqrt(2.0 / (n_win * NBINS))
    lines = channels * GROUPS * n_rec
    hbm = pl.BlockSpec(memory_space=pltpu.HBM)
    dma = pltpu.SemaphoreType.DMA
    tables = inner_table(), outer_table(), lag_table()
    return pl.pallas_call(
        functools.partial(correlate_kernel, n_win, n_chan, rows, scale),
        out_shape=jax.ShapeDtypeStruct((lines, LANES), f32),
        in_specs=[hbm] * 4,
        out_specs=pl.BlockSpec(memory_space=pltpu.VMEM),
        scratch_shapes=[
            pltpu.VMEM((rows, samples), bf16),
            *[pltpu.VMEM(t.shape, t.dtype) for t in tables],
            pltpu.VMEM((n_win, channels, 2 * NBINS), bf16),
            pltpu.VMEM((n_win, rows, 2 * NBINS), f32),
            pltpu.VMEM((n_win, n_rec, 16, 2 * NBINS), f32),
            pltpu.VMEM((n_rec * 2 * rows, 2 * NBINS), bf16),
            dma((4,)),
            *[dma((n_win,))] * 2,
            *[dma((n_win, chips))] * 4,
        ],
        compiler_params=pltpu.CompilerParams(
            collective_id=0,
            has_side_effects=True,
            vmem_limit_bytes=(20 * 2**20 + lines * LANES * 4),
        ),
        name="correlate_channels",
    )(records, *[jnp.asarray(t) for t in tables])


def spread_kernel(rows, per_shard, lines, corr, src_hbm, out_ref, src_ref, load, sem):
    count = src_ref.shape[1]
    fetch = pltpu.make_async_copy(src_hbm, src_ref, load)
    fetch.start()
    fetch.wait()

    @pl.loop(0, count)
    def _(j):
        c = j // per_shard * rows + src_ref[0, j]
        pltpu.make_async_copy(
            corr.at[pl.ds(pl.multiple_of(c * lines, lines), lines)],
            out_ref.at[pl.ds(pl.multiple_of(j * lines, lines), lines)],
            sem,
        ).start()

    pltpu.make_async_copy(out_ref, out_ref, sem).wait()


def spread(corr, source_rows, rows, n_win, n_chan):
    n_rec = rows // n_win
    count = source_rows.shape[1]
    lines = GROUPS * n_rec
    out = pl.pallas_call(
        functools.partial(spread_kernel, rows, count // n_chan, lines),
        out_shape=jax.ShapeDtypeStruct((count * lines, LANES), f32),
        in_specs=[
            pl.BlockSpec(memory_space=pltpu.VMEM),
            pl.BlockSpec(memory_space=pltpu.HBM),
        ],
        out_specs=pl.BlockSpec(memory_space=pltpu.HBM),
        scratch_shapes=[
            pltpu.SMEM(source_rows.shape, jnp.int32),
            pltpu.SemaphoreType.DMA,
            pltpu.SemaphoreType.DMA,
        ],
        compiler_params=pltpu.CompilerParams(
            vmem_limit_bytes=2**20 + corr.size * 4,
        ),
        name="spread_to_sources",
    )(corr, source_rows)
    out = out.reshape(count, GROUPS, n_rec, LANES).transpose(0, 2, 1, 3)
    return out.reshape(count, n_rec, 2 * MAXLAG)


def per_device(records, source_rows):
    n_win, n_chan = lax.axis_size("win"), lax.axis_size("chan")
    _, rows, samples = records.shape
    corr = correlated(records.reshape(rows, samples), n_win, n_chan)
    return spread(corr, source_rows, rows, n_win, n_chan)


def solution(mesh):
    in_specs = (P("win", "chan", None), P())
    out_specs = P(None, ("chan", "win"), None)
    return jax.shard_map(
        per_device, mesh=mesh, in_specs=in_specs, out_specs=out_specs, check_vma=False
    )
```

```python
import functools
import math

import jax
import jax.numpy as jnp
import ml_dtypes
import numpy as np
from jax import lax
from jax.experimental import pallas as pl
from jax.experimental.pallas import tpu as pltpu
from jax.sharding import PartitionSpec as P

S = 7680
NBINS = 512
HALF = 32
FIRST_BIN = 64
MAXLAG = 1024

INNER = 512
OUTER = S // INNER
LOW = FIRST_BIN - HALF
WIDE = 640
LANES = 128
GROUPS = 2 * MAXLAG // LANES
MESH = pl.DeviceIdType.MESH
bf16 = jnp.bfloat16
f32 = jnp.float32


def angles(left, right):
    turn = np.float32(2.0 * math.pi / S)
    return (left[:, None] * right[None, :] % S).astype(np.float32) * turn


def inner_table():
    a = angles(np.arange(INNER), LOW + np.arange(WIDE))
    return np.concatenate([np.cos(a), -np.sin(a)], axis=1).astype(ml_dtypes.bfloat16)


def outer_table():
    a = angles(INNER * np.arange(OUTER), LOW + np.arange(WIDE))
    return np.stack([np.cos(a), np.sin(a)]).astype(np.float32)


def lag_table():
    a = angles(FIRST_BIN + np.arange(NBINS), np.arange(2 * MAXLAG) - MAXLAG)
    return np.concatenate([np.cos(a), -np.sin(a)], axis=0).astype(ml_dtypes.bfloat16)


def spectra_of(x_ref, table_ref, outer_ref):
    rows = x_ref.shape[0]
    parts = [x_ref[:, i * INNER : (i + 1) * INNER] for i in range(OUTER)]
    z = jnp.dot(
        jnp.concatenate(parts, axis=0), table_ref[...], preferred_element_type=f32
    )
    re = im = None
    for i in range(OUTER):
        zr = z[i * rows : (i + 1) * rows, :WIDE]
        zi = z[i * rows : (i + 1) * rows, WIDE:]
        c = outer_ref[0, i : i + 1, :]
        s = outer_ref[1, i : i + 1, :]
        tr = zr * c + zi * s
        ti = zi * c - zr * s
        re = tr if re is None else re + tr
        im = ti if im is None else im + ti
    return re, im


def whiten(re, im):
    total = jnp.sqrt(re * re + im * im)
    first = total
    span = 1
    while span < 2 * HALF:
        total = total + pltpu.roll(total, WIDE - span, 1)
        span *= 2
    total = total + pltpu.roll(first, WIDE - span, 1)
    amplitude = total[:, :NBINS] / (2 * HALF + 1) + 1e-06
    re = pltpu.roll(re, WIDE - HALF, 1)[:, :NBINS] / amplitude
    im = pltpu.roll(im, WIDE - HALF, 1)[:, :NBINS] / amplitude
    return re.astype(bf16), im.astype(bf16)


def correlate_kernel(
    n_win,
    n_chan,
    rows,
    scale,
    x_hbm,
    table_hbm,
    outer_hbm,
    lag_hbm,
    corr,
    x_ref,
    table_ref,
    outer_ref,
    lag_ref,
    all_ref,
    own,
    wide,
    lhs,
    load,
    s1,
    r1,
    s2,
    r2,
    s3,
    r3,
):
    chips = n_chan // 2
    n_rec = rows // n_win
    lines = GROUPS * n_rec
    per_chip = 2 * rows
    win, chan = lax.axis_index("win"), lax.axis_index("chan")
    chip, core = chan // 2, chan % 2
    sibling = chip * 2 + (1 - core)

    loads = [
        pltpu.make_async_copy(src, dst, load.at[i])
        for i, (src, dst) in enumerate(
            (
                (x_hbm, x_ref),
                (table_hbm, table_ref),
                (outer_hbm, outer_ref),
                (lag_hbm, lag_ref),
            )
        )
    ]
    for c in loads:
        c.start()

    def turn(d):
        return lax.rem(win + d, n_win)

    def other(p):
        bits = [1 << b for b in range((chips - 1).bit_length())]
        return sum((chip // b + p // b) % 2 * b for b in bits)

    def peer(p):
        return other(p) * 2 + core

    barrier = pltpu.get_barrier_semaphore()
    friends = [(chan, turn(d)) for d in range(1, n_win)]
    friends += [(peer(p), win) for p in range(1, chips)] + [(sibling, win)]
    for c, w in friends:
        pl.semaphore_signal(
            barrier, inc=1, device_id={"chan": c, "win": w}, device_id_type=MESH
        )

    for c in loads[:3]:
        c.wait()
    re, im = whiten(*spectra_of(x_ref, table_ref, outer_ref))
    mine = pl.ds(pl.multiple_of(chan * rows, rows), rows)
    all_ref[win, mine, :NBINS] = re
    all_ref[win, mine, NBINS:] = im
    pl.semaphore_wait(barrier, len(friends))

    def copy(w, c, to_c, to_w, send, recv):
        block = all_ref.at[w, pl.ds(pl.multiple_of(c * rows, rows), rows)]
        return pltpu.make_async_remote_copy(
            src_ref=block,
            dst_ref=block,
            send_sem=send,
            recv_sem=recv,
            device_id={"chan": to_c, "win": to_w},
            device_id_type=MESH,
        )

    def along(d):
        return copy(win, chan, chan, turn(d), s1.at[d], r1.at[d])

    def across(d, p):
        return copy(turn(n_win - d), chan, peer(p), win, s2.at[d, p], r2.at[d, p])

    def onward(d, p):
        w, c = turn(n_win - d), peer(p)
        return copy(w, c, sibling, win, s3.at[d, p], r3.at[d, p])

    near = [p for p in range(1, chips) if p & (p - 1) == 0]
    for d in range(1, n_win):
        along(d).start()
    for d in range(n_win):
        if d:
            copy(turn(n_win - d), chan, chan, turn(d), s1.at[d], r1.at[d]).wait_recv()
        for p in range(1, chips):
            if d == 0 or p in near:
                across(d, p).start()
        onward(d, 0).start()
    for d in range(1, n_win):
        for p in range(1, chips):
            if p not in near:
                across(d, p).start()

    for w in range(n_win):
        own[w] = all_ref[w, mine, :].astype(f32)
    for w in range(n_win):
        for r in range(n_rec):
            line = own[w, pl.ds(win * n_rec + r, 1), :]
            wide[w, r] = jnp.broadcast_to(line, (16, 2 * NBINS))
    loads[3].wait()

    @pl.loop(1, chips + 1)
    def _(q):
        @pl.when(q < chips)
        def _():
            for d in range(n_win):
                w, c = turn(n_win - d), peer(q)
                copy(w, c, peer(q), win, s2.at[d, q], r2.at[d, q]).wait_recv()
                onward(d, q).start()

        p = q - 1
        there = other(p)
        for d in range(n_win):
            w, c = turn(n_win - d), there * 2 + (1 - core)
            copy(w, c, sibling, win, s3.at[d, p], r3.at[d, p]).wait_recv()

        for k in range(NBINS // LANES):
            at_re = pl.ds(k * LANES, LANES)
            at_im = pl.ds(NBINS + k * LANES, LANES)

            @pl.loop(0, per_chip // 16)
            def _(i):
                here = pl.ds(pl.multiple_of(there * per_chip + i * 16, 16), 16)
                s_re = [all_ref[w, here, at_re].astype(f32) for w in range(n_win)]
                s_im = [all_ref[w, here, at_im].astype(f32) for w in range(n_win)]
                for r in range(n_rec):
                    re = im = None
                    for w in range(n_win):
                        r_re, r_im = wide[w, r, :, at_re], wide[w, r, :, at_im]
                        a = s_re[w] * r_re + s_im[w] * r_im
                        c = s_im[w] * r_re - s_re[w] * r_im
                        re = a if re is None else re + a
                        im = c if im is None else im + c
                    to = pl.ds(pl.multiple_of(r * per_chip + i * 16, 16), 16)
                    lhs[to, at_re] = re.astype(bf16)
                    lhs[to, at_im] = im.astype(bf16)

        for n in range(GROUPS // 2):
            res = jnp.dot(
                lhs[...], lag_ref[:, n * 256 : (n + 1) * 256], preferred_element_type=f32
            )
            res = res * scale
            for h in range(2):
                for r in range(n_rec):
                    for c in range(0, per_chip, 8):
                        first = (there * per_chip + c) * lines + (2 * n + h) * n_rec + r
                        corr[pl.ds(first, 8, stride=lines), :] = res[
                            r * per_chip + c : r * per_chip + c + 8,
                            h * LANES : (h + 1) * LANES,
                        ]

    for d in range(1, n_win):
        along(d).wait_send()

    @pl.loop(1, chips)
    def _(p):
        for d in range(n_win):
            across(d, p).wait_send()

    @pl.loop(0, chips)
    def _(p):
        for d in range(n_win):
            onward(d, p).wait_send()


def in_hbm(array):
    return pltpu.with_memory_space_constraint(jnp.asarray(array), pltpu.HBM)


def correlated(records, n_win, n_chan):
    rows, samples = records.shape
    chips = n_chan // 2
    n_rec = rows // n_win
    channels = n_chan * rows
    scale = math.sqrt(2.0 / (n_win * NBINS))
    lines = channels * GROUPS * n_rec
    hbm = pl.BlockSpec(memory_space=pltpu.HBM)
    dma = pltpu.SemaphoreType.DMA
    tables = inner_table(), outer_table(), lag_table()
    return pl.pallas_call(
        functools.partial(correlate_kernel, n_win, n_chan, rows, scale),
        out_shape=jax.ShapeDtypeStruct((lines, LANES), f32),
        in_specs=[hbm] * 4,
        out_specs=pl.BlockSpec(memory_space=pltpu.VMEM),
        scratch_shapes=[
            pltpu.VMEM((rows, samples), bf16),
            *[pltpu.VMEM(t.shape, t.dtype) for t in tables],
            pltpu.VMEM((n_win, channels, 2 * NBINS), bf16),
            pltpu.VMEM((n_win, rows, 2 * NBINS), f32),
            pltpu.VMEM((n_win, n_rec, 16, 2 * NBINS), f32),
            pltpu.VMEM((n_rec * 2 * rows, 2 * NBINS), bf16),
            dma((4,)),
            *[dma((n_win,))] * 2,
            *[dma((n_win, chips))] * 4,
        ],
        compiler_params=pltpu.CompilerParams(
            collective_id=0,
            has_side_effects=True,
            vmem_limit_bytes=(20 * 2**20 + lines * LANES * 4),
        ),
        name="correlate_channels",
    )(*[in_hbm(t) for t in (records, *tables)])


def spread_kernel(rows, per_shard, lines, corr, src_hbm, out_ref, src_ref, load, sem):
    count = src_ref.shape[1]
    fetch = pltpu.make_async_copy(src_hbm, src_ref, load)
    fetch.start()
    fetch.wait()

    @pl.loop(0, count)
    def _(j):
        c = j // per_shard * rows + src_ref[0, j]
        pltpu.make_async_copy(
            corr.at[pl.ds(pl.multiple_of(c * lines, lines), lines)],
            out_ref.at[pl.ds(pl.multiple_of(j * lines, lines), lines)],
            sem,
        ).start()

    pltpu.make_async_copy(out_ref, out_ref, sem).wait()


def spread(corr, source_rows, rows, n_win, n_chan):
    n_rec = rows // n_win
    count = source_rows.shape[1]
    lines = GROUPS * n_rec
    out = pl.pallas_call(
        functools.partial(spread_kernel, rows, count // n_chan, lines),
        out_shape=jax.ShapeDtypeStruct((count * lines, LANES), f32),
        in_specs=[
            pl.BlockSpec(memory_space=pltpu.VMEM),
            pl.BlockSpec(memory_space=pltpu.HBM),
        ],
        out_specs=pl.BlockSpec(memory_space=pltpu.HBM),
        scratch_shapes=[
            pltpu.SMEM(source_rows.shape, jnp.int32),
            pltpu.SemaphoreType.DMA,
            pltpu.SemaphoreType.DMA,
        ],
        compiler_params=pltpu.CompilerParams(
            vmem_limit_bytes=2**20 + corr.size * 4,
        ),
        name="spread_to_sources",
    )(corr, in_hbm(source_rows))
    out = out.reshape(count, GROUPS, n_rec, LANES).transpose(0, 2, 1, 3)
    return out.reshape(count, n_rec, 2 * MAXLAG)


def per_device(records, source_rows):
    n_win, n_chan = lax.axis_size("win"), lax.axis_size("chan")
    _, rows, samples = records.shape
    corr = correlated(records.reshape(rows, samples), n_win, n_chan)
    return spread(corr, source_rows, rows, n_win, n_chan)


def solution(mesh):
    in_specs = (P("win", "chan", None), P())
    out_specs = P(None, ("chan", "win"), None)
    return jax.shard_map(
        per_device, mesh=mesh, in_specs=in_specs, out_specs=out_specs, check_vma=False
    )
```

```python
import functools
import math

import jax
import jax.numpy as jnp
import ml_dtypes
import numpy as np
from jax import lax
from jax.experimental import pallas as pl
from jax.experimental.pallas import tpu as pltpu
from jax.sharding import PartitionSpec as P

S = 7680
NBINS = 512
HALF = 32
FIRST_BIN = 64
MAXLAG = 1024

INNER = 512
OUTER = S // INNER
LOW = FIRST_BIN - HALF
WIDE = 640
LANES = 128
GROUPS = 2 * MAXLAG // LANES
MESH = pl.DeviceIdType.MESH
bf16 = jnp.bfloat16
f32 = jnp.float32


def angles(left, right):
    turn = np.float32(2.0 * math.pi / S)
    return (left[:, None] * right[None, :] % S).astype(np.float32) * turn


def inner_table():
    a = angles(np.arange(INNER), LOW + np.arange(WIDE))
    return np.concatenate([np.cos(a), -np.sin(a)], axis=1).astype(ml_dtypes.bfloat16)


def outer_table():
    a = angles(INNER * np.arange(OUTER), LOW + np.arange(WIDE))
    return np.stack([np.cos(a), np.sin(a)]).astype(np.float32)


def lag_table():
    a = angles(FIRST_BIN + np.arange(NBINS), np.arange(MAXLAG + LANES))
    return np.concatenate([np.cos(a), np.sin(a)], axis=0).astype(ml_dtypes.bfloat16)


def spectra_of(x_ref, table_ref, outer_ref):
    rows = x_ref.shape[0]
    parts = [x_ref[:, i * INNER : (i + 1) * INNER] for i in range(OUTER)]
    z = jnp.dot(
        jnp.concatenate(parts, axis=0), table_ref[...], preferred_element_type=f32
    )
    re = im = None
    for i in range(OUTER):
        zr = z[i * rows : (i + 1) * rows, :WIDE]
        zi = z[i * rows : (i + 1) * rows, WIDE:]
        c = outer_ref[0, i : i + 1, :]
        s = outer_ref[1, i : i + 1, :]
        tr = zr * c + zi * s
        ti = zi * c - zr * s
        re = tr if re is None else re + tr
        im = ti if im is None else im + ti
    return re, im


def whiten(re, im):
    total = jnp.sqrt(re * re + im * im)
    first = total
    span = 1
    while span < 2 * HALF:
        total = total + pltpu.roll(total, WIDE - span, 1)
        span *= 2
    total = total + pltpu.roll(first, WIDE - span, 1)
    amplitude = total[:, :NBINS] / (2 * HALF + 1) + 1e-06
    re = pltpu.roll(re, WIDE - HALF, 1)[:, :NBINS] / amplitude
    im = pltpu.roll(im, WIDE - HALF, 1)[:, :NBINS] / amplitude
    return re.astype(bf16), im.astype(bf16)


def correlate_kernel(
    n_win,
    n_chan,
    rows,
    scale,
    x_hbm,
    table_hbm,
    outer_hbm,
    lag_hbm,
    corr,
    x_ref,
    table_ref,
    outer_ref,
    lag_ref,
    all_ref,
    own,
    wide,
    lhs,
    load,
    s1,
    r1,
    s2,
    r2,
    s3,
    r3,
):
    chips = n_chan // 2
    n_rec = rows // n_win
    lines = GROUPS * n_rec
    per_chip = 2 * rows
    win, chan = lax.axis_index("win"), lax.axis_index("chan")
    chip, core = chan // 2, chan % 2
    sibling = chip * 2 + (1 - core)

    loads = [
        pltpu.make_async_copy(src, dst, load.at[i])
        for i, (src, dst) in enumerate(
            (
                (x_hbm, x_ref),
                (table_hbm, table_ref),
                (outer_hbm, outer_ref),
                (lag_hbm, lag_ref),
            )
        )
    ]
    for c in loads:
        c.start()

    def turn(d):
        return lax.rem(win + d, n_win)

    def other(p):
        bits = [1 << b for b in range((chips - 1).bit_length())]
        return sum((chip // b + p // b) % 2 * b for b in bits)

    def peer(p):
        return other(p) * 2 + core

    barrier = pltpu.get_barrier_semaphore()
    friends = [(chan, turn(d)) for d in range(1, n_win)]
    friends += [(peer(p), win) for p in range(1, chips)] + [(sibling, win)]
    for c, w in friends:
        pl.semaphore_signal(
            barrier, inc=1, device_id={"chan": c, "win": w}, device_id_type=MESH
        )

    for c in loads[:3]:
        c.wait()
    re, im = whiten(*spectra_of(x_ref, table_ref, outer_ref))
    mine = pl.ds(pl.multiple_of(chan * rows, rows), rows)
    all_ref[win, mine, :NBINS] = re
    all_ref[win, mine, NBINS:] = im
    pl.semaphore_wait(barrier, len(friends))

    def copy(w, c, to_c, to_w, send, recv):
        block = all_ref.at[w, pl.ds(pl.multiple_of(c * rows, rows), rows)]
        return pltpu.make_async_remote_copy(
            src_ref=block,
            dst_ref=block,
            send_sem=send,
            recv_sem=recv,
            device_id={"chan": to_c, "win": to_w},
            device_id_type=MESH,
        )

    def along(d):
        return copy(win, chan, chan, turn(d), s1.at[d], r1.at[d])

    def across(d, p):
        return copy(turn(n_win - d), chan, peer(p), win, s2.at[d, p], r2.at[d, p])

    def onward(d, p):
        w, c = turn(n_win - d), peer(p)
        return copy(w, c, sibling, win, s3.at[d, p], r3.at[d, p])

    near = [p for p in range(1, chips) if p & (p - 1) == 0]
    for d in range(1, n_win):
        along(d).start()
    for d in range(n_win):
        if d:
            copy(turn(n_win - d), chan, chan, turn(d), s1.at[d], r1.at[d]).wait_recv()
        for p in range(1, chips):
            if d == 0 or p in near:
                across(d, p).start()
        onward(d, 0).start()
    for d in range(1, n_win):
        for p in range(1, chips):
            if p not in near:
                across(d, p).start()

    for w in range(n_win):
        own[w] = all_ref[w, mine, :].astype(f32)
    for w in range(n_win):
        for r in range(n_rec):
            line = own[w, pl.ds(win * n_rec + r, 1), :]
            wide[w, r] = jnp.broadcast_to(line, (16, 2 * NBINS))
    loads[3].wait()

    @pl.loop(1, chips + 1)
    def _(q):
        @pl.when(q < chips)
        def _():
            for d in range(n_win):
                w, c = turn(n_win - d), peer(q)
                copy(w, c, peer(q), win, s2.at[d, q], r2.at[d, q]).wait_recv()
                onward(d, q).start()

        p = q - 1
        there = other(p)
        for d in range(n_win):
            w, c = turn(n_win - d), there * 2 + (1 - core)
            copy(w, c, sibling, win, s3.at[d, p], r3.at[d, p]).wait_recv()

        for k in range(NBINS // LANES):
            at_re = pl.ds(k * LANES, LANES)
            at_im = pl.ds(NBINS + k * LANES, LANES)

            @pl.loop(0, per_chip // 16)
            def _(i):
                here = pl.ds(pl.multiple_of(there * per_chip + i * 16, 16), 16)
                s_re = [all_ref[w, here, at_re].astype(f32) for w in range(n_win)]
                s_im = [all_ref[w, here, at_im].astype(f32) for w in range(n_win)]
                for r in range(n_rec):
                    re = im = None
                    for w in range(n_win):
                        r_re, r_im = wide[w, r, :, at_re], wide[w, r, :, at_im]
                        a = s_re[w] * r_re + s_im[w] * r_im
                        c = s_im[w] * r_re - s_re[w] * r_im
                        re = a if re is None else re + a
                        im = c if im is None else im + c
                    to = pl.ds(pl.multiple_of(r * per_chip + i * 16, 16), 16)
                    lhs[to, at_re] = re.astype(bf16)
                    lhs[to, at_im] = im.astype(bf16)

        def at_lags(first, count):
            at = slice(first, first + count)
            even = jnp.dot(
                lhs[:, :NBINS], lag_ref[:NBINS, at], preferred_element_type=f32
            )
            odd = jnp.dot(
                lhs[:, NBINS:], lag_ref[NBINS:, at], preferred_element_type=f32
            )
            return even * scale, odd * scale

        def store(group, block):
            for r in range(n_rec):
                for c in range(0, per_chip, 8):
                    first = (there * per_chip + c) * lines + group * n_rec + r
                    corr[pl.ds(first, 8, stride=lines), :] = block[
                        r * per_chip + c : r * per_chip + c + 8
                    ]

        shape = (n_rec * per_chip, LANES)
        lane = lax.broadcasted_iota(jnp.int32, shape, 1)
        mirror = jnp.where(lane == 0, 0, LANES - lane)

        def mirrored(block):
            return jnp.take_along_axis(block, mirror, axis=1)

        even, odd = at_lags(MAXLAG, LANES)
        later = mirrored(even + odd)
        half = GROUPS // 2
        for n in range(half // 2 - 1, -1, -1):
            evens, odds = at_lags(n * 256, 256)
            for h in (1, 0):
                even = evens[:, h * LANES : (h + 1) * LANES]
                odd = odds[:, h * LANES : (h + 1) * LANES]
                group = 2 * n + h
                store(half + group, even - odd)
                block = mirrored(even + odd)
                store(half - 1 - group, jnp.where(lane == 0, later, block))
                later = block

    for d in range(1, n_win):
        along(d).wait_send()

    @pl.loop(1, chips)
    def _(p):
        for d in range(n_win):
            across(d, p).wait_send()

    @pl.loop(0, chips)
    def _(p):
        for d in range(n_win):
            onward(d, p).wait_send()


def in_hbm(array):
    return pltpu.with_memory_space_constraint(jnp.asarray(array), pltpu.HBM)


def correlated(records, n_win, n_chan):
    rows, samples = records.shape
    chips = n_chan // 2
    n_rec = rows // n_win
    channels = n_chan * rows
    scale = math.sqrt(2.0 / (n_win * NBINS))
    lines = channels * GROUPS * n_rec
    hbm = pl.BlockSpec(memory_space=pltpu.HBM)
    dma = pltpu.SemaphoreType.DMA
    tables = inner_table(), outer_table(), lag_table()
    return pl.pallas_call(
        functools.partial(correlate_kernel, n_win, n_chan, rows, scale),
        out_shape=jax.ShapeDtypeStruct((lines, LANES), f32),
        in_specs=[hbm] * 4,
        out_specs=pl.BlockSpec(memory_space=pltpu.VMEM),
        scratch_shapes=[
            pltpu.VMEM((rows, samples), bf16),
            *[pltpu.VMEM(t.shape, t.dtype) for t in tables],
            pltpu.VMEM((n_win, channels, 2 * NBINS), bf16),
            pltpu.VMEM((n_win, rows, 2 * NBINS), f32),
            pltpu.VMEM((n_win, n_rec, 16, 2 * NBINS), f32),
            pltpu.VMEM((n_rec * 2 * rows, 2 * NBINS), bf16),
            dma((4,)),
            *[dma((n_win,))] * 2,
            *[dma((n_win, chips))] * 4,
        ],
        compiler_params=pltpu.CompilerParams(
            collective_id=0,
            has_side_effects=True,
            vmem_limit_bytes=(20 * 2**20 + lines * LANES * 4),
        ),
        name="correlate_channels",
    )(*[in_hbm(t) for t in (records, *tables)])


def spread_kernel(rows, per_shard, lines, corr, src_hbm, out_ref, src_ref, load, sem):
    count = src_ref.shape[1]
    fetch = pltpu.make_async_copy(src_hbm, src_ref, load)
    fetch.start()
    fetch.wait()

    @pl.loop(0, count, unroll=8)
    def _(j):
        c = j // per_shard * rows + src_ref[0, j]
        pltpu.make_async_copy(
            corr.at[pl.ds(pl.multiple_of(c * lines, lines), lines)],
            out_ref.at[pl.ds(pl.multiple_of(j * lines, lines), lines)],
            sem,
        ).start()

    pltpu.make_async_copy(out_ref, out_ref, sem).wait()


def spread(corr, source_rows, rows, n_win, n_chan):
    n_rec = rows // n_win
    count = source_rows.shape[1]
    lines = GROUPS * n_rec
    out = pl.pallas_call(
        functools.partial(spread_kernel, rows, count // n_chan, lines),
        out_shape=jax.ShapeDtypeStruct((count * lines, LANES), f32),
        in_specs=[
            pl.BlockSpec(memory_space=pltpu.VMEM),
            pl.BlockSpec(memory_space=pltpu.HBM),
        ],
        out_specs=pl.BlockSpec(memory_space=pltpu.HBM),
        scratch_shapes=[
            pltpu.SMEM(source_rows.shape, jnp.int32),
            pltpu.SemaphoreType.DMA,
            pltpu.SemaphoreType.DMA,
        ],
        compiler_params=pltpu.CompilerParams(
            vmem_limit_bytes=2**20 + corr.size * 4,
        ),
        name="spread_to_sources",
    )(corr, source_rows)
    out = out.reshape(count, GROUPS, n_rec, LANES).transpose(0, 2, 1, 3)
    return out.reshape(count, n_rec, 2 * MAXLAG)


def per_device(records, source_rows):
    n_win, n_chan = lax.axis_size("win"), lax.axis_size("chan")
    _, rows, samples = records.shape
    corr = correlated(records.reshape(rows, samples), n_win, n_chan)
    return spread(corr, source_rows, rows, n_win, n_chan)


def solution(mesh):
    in_specs = (P("win", "chan", None), P())
    out_specs = P(None, ("chan", "win"), None)
    return jax.shard_map(
        per_device, mesh=mesh, in_specs=in_specs, out_specs=out_specs, check_vma=False
    )
```
